512 devices in a mesh: ctx: 64 (over x, y, core), tp: 8 (over z).
Axes of the slice: x: 4, y: 8, z: 8, core: 2. Of those that a mesh axis runs over, the one named last changes fastest.
Arguments:
- hidden: bfloat16 [2, 64, 8192], P(None, None, 'ctx'), may hold values from -9 to 9
- qkv_weight: bfloat16 [8192, 10240], P('ctx', 'tp'), may hold values from -0.0625 to 0.0625
- qkv_bias: bfloat16 [10240], P('tp'), may hold values from -4 to 4
- out_weight: bfloat16 [8192, 8192], P('tp', 'ctx'), may hold values from -0.0625 to 0.0625
- prefix_cache: bfloat16 [8, 16384, 2048], P(None, 'ctx', 'tp'), may hold values from -12 to 12
- tail_cache: bfloat16 [4096, 1, 16, 2048], P('ctx', None, None, 'tp'), may hold values from -12 to 12
- parents: int32 [2, 64], replicated, may hold values from 0 to 63, as said below
- start_dev: int32 [3, 64], replicated, may hold values from 0 to 63, as said below
Outputs:
- attended: bfloat16 [2, 64, 8192], P(None, 'tp', 'ctx')
- tail_out: bfloat16 [4096, 1, 16, 2048], P('ctx', None, None, 'tp')
The draws below stay inside these ranges and needn't reach their ends.
Inputs may be any that keep to these rules, and one draw needn't show every extreme that they name: parents[s, c] is a beam of the same prompt as c, that is with the same c // 8. For each step s, among the values (start_dev[s + 1, c] - start_dev[s, parents[s, c]]) mod 64 over all beams c, a quarter of the residues are taken by exactly 2 beams each, half by 1 beams each, and the rest by none.
All inputs are finite; a program needn't handle non-finite values.
Results may differ from the reference program's by a relative error of at most 0.019.
Values may be sent and summed in bfloat16 or wider, within the bound.
No kernel may reach another device: no remote copies, remote signals or barrier semaphores. Data moves between devices by JAX's collectives and lax.ppermute only.
A program may use at most 128 MiB of HBM per device.

```python
import jax
import jax.numpy as jnp
from jax import lax

D = 8192
H = 64
KVH = 8
HD = 128
GROUP = 8
BW = 8
PROMPTS = 8
PAGE = 16
TPD = 1
STEPS = 2
BEAMS = 64
PREFIX = 16384
TAIL_PAGES = 64
TAIL = 1024
N_CTX = 64


def parent_table(key):
    base_key = jax.random.fold_in(key, 101)
    draw_one = jax.random.randint(base_key, (STEPS, BEAMS), 0, BW, dtype=jnp.int32)
    draw_two = jax.random.randint(jax.random.fold_in(base_key, 1), (STEPS, BEAMS), 0, BW, dtype=jnp.int32)
    group_base = jnp.arange(BEAMS, dtype=jnp.int32) // BW * BW
    return (group_base[None, :] + jnp.minimum(draw_one, draw_two)).astype(jnp.int32)


def draw_parents(key, part):
    return parent_table(key)


def draw_start_dev(key, part):
    parent = parent_table(key)
    key = jax.random.fold_in(key, 7)
    per_value = BEAMS // N_CTX
    row_list = [jax.random.randint(key, (BEAMS,), 0, N_CTX, dtype=jnp.int32)]
    for step_idx in range(STEPS):
        beam_order = jax.random.permutation(jax.random.fold_in(key, 10 + step_idx), BEAMS).astype(jnp.int32)
        bucket = beam_order // per_value
        bucket = jnp.where(bucket < N_CTX // 2, bucket % (N_CTX // 4), bucket)
        spread = jax.random.permutation(jax.random.fold_in(key, 20 + step_idx), N_CTX).astype(jnp.int32)
        offsets = spread[bucket]
        row_list.append((row_list[-1][parent[step_idx]] + offsets) % N_CTX)
    return jnp.stack(row_list).astype(jnp.int32)


def draw_qkv_bias(key, part):
    key = jax.random.fold_in(key, 11)
    noise_part = 0.5 * jax.random.normal(key, (KVH, GROUP + 2, HD), jnp.float32)
    bias_table = noise_part
    return jnp.clip(bias_table, -4.0, 4.0).reshape(KVH * (GROUP + 2) * HD).astype(jnp.bfloat16)


def draw_prefix_cache(key, part):
    key = jax.random.fold_in(key, 13)
    base_draw = jnp.clip(2.0 * jax.random.normal(key, (PROMPTS, PREFIX, KVH, 2, HD), jnp.float32), -12.0, 12.0)
    return base_draw.reshape(PROMPTS, PREFIX, KVH * 2 * HD).astype(jnp.bfloat16)


def shard_levels(own_key, extent, split, least, high):
    factor_of = 1.0
    for dim, blocks in split:
        heights = jax.random.uniform(jax.random.fold_in(jax.random.fold_in(own_key, 6), dim), (blocks,), jnp.float32, least / len(split), high / len(split))
        factor_of = factor_of * jnp.repeat(jnp.exp(heights), extent[dim] // blocks).reshape((-1,) + (1,) * (len(extent) - 1 - dim))
    return factor_of


def noise(key, extent, deviation, limit, pieces=(), kind=jnp.bfloat16):
    result = jax.random.normal(key, extent, jnp.float32) * deviation
    if len(pieces) > 0:
        result = shard_levels(key, extent, pieces, -0.22, 0.18) * result
    return jnp.clip(result, min=-limit, max=limit).astype(kind)


def setup_inputs(seed: int = 0) -> dict:
    key_of = jax.random.split(jax.random.key(seed), 9)
    return {
        "hidden": noise(key_of[0], (STEPS, BEAMS, D), 1.5, 9.0, ((2, 64),)),
        "qkv_weight": noise(key_of[1], (D, KVH * (GROUP + 2) * HD), D ** -0.5, 0.0625, ((0, 64), (1, 8))),
        "qkv_bias": draw_qkv_bias(jax.random.fold_in(key_of[8], 71), 0),
        "out_weight": noise(key_of[3], (H * HD, D), (H * HD) ** -0.5, 0.0625, ((0, 8), (1, 64))),
        "prefix_cache": draw_prefix_cache(jax.random.fold_in(key_of[8], 71), 0),
        "tail_cache": noise(key_of[5], (N_CTX * BEAMS, TPD, PAGE, KVH * 2 * HD), 2.0, 12.0, ((0, 64), (3, 8))),
        "parents": draw_parents(jax.random.fold_in(key_of[8], 71), 0),
        "start_dev": draw_start_dev(jax.random.fold_in(key_of[8], 71), 0),
    }


ROPE_BASE = 1000000.0


def rope_tables(position):
    half_dim = HD // 2
    frequency = ROPE_BASE ** (-(jnp.arange(half_dim, dtype=jnp.float32) * 2.0) / HD)
    angles = position * frequency
    return jnp.cos(angles), jnp.sin(angles)


def rotate(vector, cosine, sine_part):
    half_dim = HD // 2
    lower_half = vector[..., :half_dim]
    upper_half = vector[..., half_dim:]
    return jnp.concatenate([lower_half * cosine - upper_half * sine_part, upper_half * cosine + lower_half * sine_part], axis=-1)


def reference(hidden, qkv_weight, qkv_bias, out_weight, prefix_cache, tail_cache, parents, start_dev):
    row_width = KVH * 2 * HD
    tail_pool = tail_cache.reshape(N_CTX, BEAMS, TPD, PAGE, row_width)
    device_ids = jnp.arange(N_CTX, dtype=jnp.int32)
    page_ids = jnp.arange(TAIL_PAGES, dtype=jnp.int32)
    token_ids = jnp.arange(TAIL, dtype=jnp.int32)
    score_scale = HD ** -0.5
    results = []
    for step_idx in range(STEPS):
        projected = jnp.dot(hidden[step_idx], qkv_weight, preferred_element_type=jnp.float32) + qkv_bias.astype(jnp.float32)
        projected = projected.reshape(BEAMS, KVH, GROUP + 2, HD)
        position = PREFIX + TAIL - STEPS + step_idx
        cosine, sine_part = rope_tables(position)
        queries = rotate(projected[:, :, :GROUP], cosine, sine_part).astype(jnp.bfloat16)
        key_new = rotate(projected[:, :, GROUP], cosine, sine_part).astype(jnp.bfloat16)
        value_new = projected[:, :, GROUP + 1].astype(jnp.bfloat16)
        parent = parents[step_idx]
        new_start = start_dev[step_idx + 1]
        offsets = (new_start - start_dev[step_idx][parent]) % N_CTX
        source_dev = (device_ids[:, None] - offsets[None, :]) % N_CTX
        tail_pool = tail_pool[source_dev, parent[None, :]]
        owner_dev = (new_start - 1) % N_CTX
        new_entry = jnp.stack([key_new, value_new], axis=2).reshape(BEAMS, row_width)
        in_row = PAGE - STEPS + step_idx
        own_page = (device_ids[:, None] == owner_dev[None, :])[:, :, None]
        tail_pool = tail_pool.at[:, :, TPD - 1, in_row].set(jnp.where(own_page, new_entry[None], tail_pool[:, :, TPD - 1, in_row]))
        valid = token_ids <= TAIL - STEPS + step_idx

        def one_prompt(prompt_idx):
            beam_ids = prompt_idx * BW + jnp.arange(BW, dtype=jnp.int32)
            holder = (page_ids[None, :] + new_start[beam_ids][:, None]) % N_CTX
            tail_rows = tail_pool[holder, beam_ids[:, None], (page_ids // N_CTX)[None, :]]
            tail_rows = tail_rows.reshape(BW, TAIL, KVH, 2, HD).astype(jnp.float32)
            prefix_rows = lax.dynamic_index_in_dim(prefix_cache, prompt_idx, 0, keepdims=False)
            prefix_rows = prefix_rows.reshape(PREFIX, KVH, 2, HD).astype(jnp.float32)
            grouped = lax.dynamic_slice_in_dim(queries, prompt_idx * BW, BW, 0).astype(jnp.float32)
            prefix_scores = jnp.einsum("bkgd,nkd->bkgn", grouped, prefix_rows[:, :, 0]) * score_scale
            tail_scores = jnp.einsum("bkgd,bnkd->bkgn", grouped, tail_rows[:, :, :, 0]) * score_scale
            tail_scores = jnp.where(valid, tail_scores, -jnp.inf)
            row_max = jnp.maximum(jnp.max(prefix_scores, axis=-1), jnp.max(tail_scores, axis=-1))[..., None]
            prefix_weights = jnp.exp(prefix_scores - row_max)
            tail_weights = jnp.exp(tail_scores - row_max)
            denominator = jnp.sum(prefix_weights, axis=-1) + jnp.sum(tail_weights, axis=-1)
            prefix_low = lax.optimization_barrier(prefix_weights.astype(jnp.bfloat16)).astype(jnp.float32)
            tail_low = lax.optimization_barrier(tail_weights.astype(jnp.bfloat16)).astype(jnp.float32)
            weighted = jnp.einsum("bkgn,nkd->bkgd", prefix_low, prefix_rows[:, :, 1])
            weighted = weighted + jnp.einsum("bkgn,bnkd->bkgd", tail_low, tail_rows[:, :, :, 1])
            return (weighted / denominator[..., None]).astype(jnp.bfloat16)

        attention = lax.map(one_prompt, jnp.arange(PROMPTS, dtype=jnp.int32))
        attention = attention.reshape(BEAMS, H * HD)
        results.append(jnp.dot(attention, out_weight, preferred_element_type=jnp.float32).astype(jnp.bfloat16))
    return jnp.stack(results), tail_pool.reshape(N_CTX * BEAMS, TPD, PAGE, row_width)
```

```python
import functools

import jax
import jax.numpy as jnp
import numpy as np
from jax import lax
from jax.experimental import pallas as pl
from jax.experimental.pallas import tpu as pltpu
from jax.sharding import PartitionSpec as P

HD = 128
BW = 8
GROUP = 8
STEPS = 2
ROWS = STEPS * BW
PAGE = 16
CTX = 64
LX, LY, LC = 4, 8, 2
POSITION = 17406
PACK = ROWS + 8
F32, BF16 = jnp.float32, jnp.bfloat16

XC_GROUPS = [[(x * LY + y) * LC + c for x in range(LX) for c in range(LC)] for y in range(LY)]
Y_GROUPS = [[(x * LY + y) * LC + c for y in range(LY)] for x in range(LX) for c in range(LC)]

VMEM = pl.BlockSpec(memory_space=pltpu.VMEM)
SMEM = pl.BlockSpec(memory_space=pltpu.SMEM)
ANY = pl.BlockSpec(memory_space=pl.ANY)
PARAMS = pltpu.CompilerParams(vmem_limit_bytes=32 * 1024 * 1024)


def rope_rows():
    half = HD // 2
    frequency = 1000000.0 ** (-(np.arange(half) * 2.0) / HD)
    cos_of, sin_of = [], []
    for s in range(STEPS):
        angles = (POSITION + s) * frequency
        cos_of.append(np.concatenate([np.cos(angles), np.cos(angles)]))
        sin_of.append(np.concatenate([-np.sin(angles), np.sin(angles)]))
    cosine = np.zeros((GROUP, PACK, HD), np.float32)
    sine = np.zeros((GROUP, PACK, HD), np.float32)
    for h in range(GROUP):
        for s in range(STEPS):
            cosine[h, s * BW : (s + 1) * BW] = cos_of[s]
            sine[h, s * BW : (s + 1) * BW] = sin_of[s]
        if h % 2 == 0:
            cosine[h, ROWS:] = cos_of[h // 2 % 2]
            sine[h, ROWS:] = sin_of[h // 2 % 2]
        else:
            cosine[h, ROWS:] = 1.0
    return cosine, sine


def project_kernel(hidden_ref, weight_ref, out_ref):
    prompts = hidden_ref.shape[1] // BW
    steps = [hidden_ref[s].astype(F32) for s in range(STEPS)]
    rows = [steps[s][p * BW : (p + 1) * BW] for p in range(prompts) for s in range(STEPS)]
    hidden = jnp.concatenate(rows, axis=0).astype(BF16)
    for col in range(GROUP + 2):
        part = jnp.dot(
            hidden, weight_ref[:, col * HD : (col + 1) * HD], preferred_element_type=F32
        )
        for p in range(prompts):
            tile = part[p * ROWS : (p + 1) * ROWS]
            if col < GROUP:
                out_ref[p * GROUP + col, :ROWS, :] = tile.astype(BF16)
            else:
                for h in range(GROUP):
                    if h % 2 == col - GROUP:
                        s = h // 2 % 2
                        out_ref[p * GROUP + h, ROWS:, :] = tile[s * BW : (s + 1) * BW].astype(BF16)


def rotate_kernel(parts_ref, bias_ref, cos_ref, sin_ref, out_ref):
    h = lax.rem(lax.axis_index("ctx"), GROUP)
    total = jnp.sum(parts_ref[...].astype(F32), axis=0)
    bias = bias_ref[...].astype(F32)
    line = lax.broadcasted_iota(jnp.int32, bias.shape, 0)
    q_bias = jnp.sum(jnp.where(line == h, bias, 0.0), axis=0, keepdims=True)
    kv_bias = jnp.sum(jnp.where(line == GROUP + lax.rem(h, 2), bias, 0.0), axis=0, keepdims=True)
    row = lax.broadcasted_iota(jnp.int32, total.shape, 0)
    total = total + jnp.where(row < ROWS, q_bias, kv_bias)
    turned = total * cos_ref[h] + pltpu.roll(total, HD // 2, 1) * sin_ref[h]
    out_ref[...] = jnp.broadcast_to(turned.astype(BF16)[None], out_ref.shape)


def attend_kernel(parents_ref, start_ref, shared_ref, prefix_ref, tail_ref, out_ref):
    me = lax.axis_index("ctx")
    prompts = prefix_ref.shape[0]
    scale = HD**-0.5
    contract = (((1,), (1,)), ((), ()))
    lane = lax.broadcasted_iota(jnp.int32, (ROWS, HD), 1)
    row = lax.broadcasted_iota(jnp.int32, (ROWS, HD), 0)
    lane_full = lax.broadcasted_iota(jnp.int32, (GROUP * ROWS, HD), 1)

    def spread(mask):
        return jnp.concatenate([mask] * GROUP, axis=0)

    for p in range(prompts):
        query = shared_ref[p * GROUP : (p + 1) * GROUP, :ROWS, :].reshape(GROUP * ROWS, HD)
        new_key = jnp.concatenate(
            [shared_ref[p * GROUP + 2 * s, ROWS:, :].astype(F32) for s in range(STEPS)]
            + [jnp.zeros((HD - ROWS, HD), F32)],
            axis=0,
        ).astype(BF16)
        new_value = jnp.concatenate(
            [shared_ref[p * GROUP + 2 * s + 1, ROWS:, :].astype(F32) for s in range(STEPS)]
            + [jnp.zeros((HD - ROWS, HD), F32)],
            axis=0,
        ).astype(BF16)
        tail = tail_ref[p * BW : (p + 1) * BW].reshape(BW * PAGE, 2 * HD)

        holder = jnp.zeros((ROWS, HD), jnp.int32)
        first_new = jnp.zeros((ROWS, HD), jnp.int32)
        stale = lane < 0
        for b in range(BW):
            near = parents_ref[1, p * BW + b]
            holder = jnp.where(row == b, parents_ref[0, p * BW + b] - p * BW, holder)
            holder = jnp.where(row == BW + b, parents_ref[0, near] - p * BW, holder)
            first_new = jnp.where(row == b, b, first_new)
            first_new = jnp.where(row == BW + b, near - p * BW, first_new)
            last_page = lax.rem(me - start_ref[0, p * BW + b] + 2 * CTX, CTX) == CTX - 1
            cut = jnp.where(last_page, PAGE - STEPS, PAGE)
            stale = stale | ((lane // PAGE == b) & (lane % PAGE >= cut))
        second_new = jnp.where(row < BW, first_new, row)
        old_seen = (lane // PAGE == holder) & jnp.logical_not(stale)
        owner = jnp.where(me == p * BW, 1, 0)
        new_seen = ((lane == first_new) | (lane == second_new)) & (owner == 1)

        old_bias = spread(jnp.where(old_seen, 0.0, -jnp.inf))
        new_bias = spread(jnp.where(new_seen, 0.0, -jnp.inf))
        s_pre = (
            lax.dot_general(query, prefix_ref[p, :, :HD], contract, preferred_element_type=F32)
            * scale
        )
        s_old = (
            lax.dot_general(query, tail[:, :HD], contract, preferred_element_type=F32) * scale
            + old_bias
        )
        s_new = (
            lax.dot_general(query, new_key, contract, preferred_element_type=F32) * scale
            + new_bias
        )
        peak = jnp.maximum(
            jnp.max(s_pre, axis=1, keepdims=True),
            jnp.max(jnp.maximum(s_old, s_new), axis=1, keepdims=True),
        )
        w_pre = jnp.exp(s_pre - peak)
        w_old = jnp.exp(s_old - peak)
        w_new = jnp.exp(s_new - peak)
        total = jnp.sum(w_pre, axis=1, keepdims=True) + jnp.sum(w_old + w_new, axis=1, keepdims=True)
        mixed = (
            jnp.dot(w_pre.astype(BF16), prefix_ref[p, :, HD:], preferred_element_type=F32)
            + jnp.dot(w_old.astype(BF16), tail[:, HD:], preferred_element_type=F32)
            + jnp.dot(w_new.astype(BF16), new_value, preferred_element_type=F32)
        )
        out_ref[p * GROUP : (p + 1) * GROUP, :ROWS, :] = mixed.astype(BF16).reshape(
            GROUP, ROWS, HD
        )

        def split(value):
            high = value.astype(BF16).astype(F32)
            rest = value - high
            mid = rest.astype(BF16).astype(F32)
            return high, mid, rest - mid

        table = jnp.zeros((GROUP * ROWS, HD), F32)
        for k, piece in enumerate(split(peak) + split(total)):
            table = jnp.where(lane_full == k, piece, table)
        stats = table.T[:8].astype(BF16)
        for h in range(GROUP):
            out_ref[p * GROUP + h, ROWS:, :] = stats


def merge_kernel(parts_ref, out_ref, scale_ref):
    h = lax.rem(lax.axis_index("ctx"), GROUP)
    stats = parts_ref[:, ROWS:, :].astype(F32)
    kind = lax.broadcasted_iota(jnp.int32, stats.shape, 1)
    peak = jnp.sum(jnp.where(kind < 3, stats, 0.0), axis=1)
    total = jnp.sum(jnp.where((kind >= 3) & (kind < 6), stats, 0.0), axis=1)
    factor = jnp.exp(peak - jnp.max(peak, axis=0, keepdims=True))
    factor = factor / jnp.sum(total * factor, axis=0, keepdims=True)
    factor = jnp.concatenate([factor, jnp.zeros((HD - CTX, HD), F32)], axis=0)
    scale_ref[...] = factor.T
    mine = scale_ref[pl.ds(pl.multiple_of(h * ROWS, ROWS), ROWS), :]
    acc = jnp.zeros((ROWS, HD), F32)
    for k in range(CTX):
        acc = acc + mine[:, k : k + 1] * parts_ref[k, :ROWS, :].astype(F32)
    out_ref[...] = jnp.broadcast_to(acc.astype(BF16)[None], out_ref.shape)


def output_kernel(heads_ref, weight_ref, out_ref):
    prompts = out_ref.shape[0]
    acc = jnp.zeros((prompts * ROWS, HD), F32)
    for h in range(GROUP):
        head = jnp.concatenate([heads_ref[p * GROUP + h] for p in range(prompts)], axis=0)
        acc = acc + jnp.dot(
            head, weight_ref[h * HD : (h + 1) * HD, :], preferred_element_type=F32
        )
    out_ref[...] = acc.astype(BF16).reshape(out_ref.shape)


def source_of(parents_ref, start_ref, c):
    far = parents_ref[0, parents_ref[1, c]]
    return far, lax.rem(start_ref[2, c] - start_ref[0, far] + CTX, CTX)


def pick_xc_kernel(parents_ref, start_ref, pages_ref, out_ref, sems):
    me = lax.axis_index("ctx")
    core, y, x = lax.rem(me, LC), lax.rem(me // LC, LY), me // (LC * LY)
    beams = out_ref.shape[0]

    def copy(c):
        far, shift = source_of(parents_ref, start_ref, c)
        s_core, s_y, s_x = lax.rem(shift, LC), lax.rem(shift // LC, LY), shift // (LC * LY)
        from_core = lax.rem(core - s_core + LC, LC)
        carry_y = (from_core + s_core) // LC
        carry_x = (y + s_y + carry_y) // LY
        from_x = lax.rem(x - s_x - carry_x + 2 * LX, LX)
        return pltpu.make_async_copy(
            pages_ref.at[(from_x * LC + from_core) * beams + far], out_ref.at[c], sems.at[c]
        )

    def start(c, _):
        copy(c).start()
        return 0

    def wait(c, _):
        pltpu.make_async_copy(pages_ref.at[0], out_ref.at[c], sems.at[c]).wait()
        return 0

    lax.fori_loop(0, beams, start, 0)
    lax.fori_loop(0, beams, wait, 0)


def finish_tail_kernel(parents_ref, start_ref, pages_ref, shared_ref, out_ref, fresh, sems):
    me = lax.axis_index("ctx")
    core, y = lax.rem(me, LC), lax.rem(me // LC, LY)
    beams = out_ref.shape[0]

    def start(c, _):
        _, shift = source_of(parents_ref, start_ref, c)
        s_core, s_y = lax.rem(shift, LC), lax.rem(shift // LC, LY)
        from_core = lax.rem(core - s_core + LC, LC)
        from_y = lax.rem(y - s_y - (from_core + s_core) // LC + 2 * LY, LY)
        pltpu.make_async_copy(
            pages_ref.at[from_y * beams + c], out_ref.at[c], sems.at[c]
        ).start()
        return 0

    def wait(c, _):
        pltpu.make_async_copy(pages_ref.at[0], out_ref.at[c], sems.at[c]).wait()
        return 0

    lax.fori_loop(0, beams, start, 0)
    for s in range(STEPS):
        for p in range(beams // BW):
            for kv in range(2):
                entry = shared_ref[p * GROUP + 2 * s + kv, ROWS:, :].astype(F32)
                fresh[s, p * BW : (p + 1) * BW, :, kv * HD : (kv + 1) * HD] = entry[:, None, :]
    lax.fori_loop(0, beams, wait, 0)

    def append(c, _):
        @pl.when(lax.rem(start_ref[2, c] - 1 + CTX, CTX) == me)
        def _():
            page = out_ref[c].astype(F32)
            line = lax.broadcasted_iota(jnp.int32, page.shape, 0)
            page = jnp.where(line == PAGE - 2, fresh[0, parents_ref[1, c]], page)
            page = jnp.where(line == PAGE - 1, fresh[1, c], page)
            out_ref[c] = page.astype(BF16)

        return 0

    lax.fori_loop(0, beams, append, 0)


def call(kernel, shape, in_specs, scratch=(), cost=None, dtype=BF16):
    return pl.pallas_call(
        kernel,
        out_shape=jax.ShapeDtypeStruct(shape, dtype),
        in_specs=in_specs,
        out_specs=VMEM,
        scratch_shapes=list(scratch),
        compiler_params=PARAMS,
        cost_estimate=cost,
    )


def per_device(
    hidden, qkv_weight, qkv_bias, out_weight, prefix_cache, tail_cache, parents, start_dev
):
    prompts = prefix_cache.shape[0]
    beams = prompts * BW
    pages = tail_cache.reshape(beams, PAGE, 2 * HD)
    cosine, sine = rope_rows()
    swap = functools.partial(lax.all_to_all, split_axis=0, concat_axis=0, tiled=True)

    wide = lax.all_gather(pages, "ctx", axis_index_groups=XC_GROUPS, tiled=True)

    parts = call(project_kernel, (CTX, PACK, HD), [VMEM] * 2)(hidden, qkv_weight)
    parts = swap(parts, "ctx")
    mine = call(rotate_kernel, (CTX, PACK, HD), [VMEM] * 4)(
        parts, qkv_bias.reshape(GROUP + 2, HD), cosine, sine
    )
    shared = swap(mine, "ctx")
    parts = call(attend_kernel, (CTX, PACK, HD), [SMEM] * 2 + [VMEM] * 3)(
        parents, start_dev, shared, prefix_cache, pages
    )
    parts, wide = lax.optimization_barrier((parts, wide))

    moved = call(
        pick_xc_kernel,
        (beams, PAGE, 2 * HD),
        [SMEM] * 2 + [ANY],
        [pltpu.SemaphoreType.DMA((beams,))],
    )(parents, start_dev, wide)
    deep = lax.all_gather(moved, "ctx", axis_index_groups=Y_GROUPS, tiled=True)

    parts = swap(parts, "ctx")
    merged = call(
        merge_kernel, (CTX, ROWS, HD), [VMEM], [pltpu.VMEM((HD, HD), F32)]
    )(parts)
    heads = swap(merged, "ctx")
    share = call(output_kernel, (prompts, ROWS, HD), [VMEM] * 2)(heads, out_weight)
    share = swap(share, "tp")
    share, deep = lax.optimization_barrier((share, deep))
    attended = jnp.sum(share.astype(F32), axis=0).astype(BF16).reshape(STEPS, BW, HD)
    tail_out = call(
        finish_tail_kernel,
        (beams, PAGE, 2 * HD),
        [SMEM] * 2 + [ANY, VMEM],
        [
            pltpu.VMEM((STEPS, beams, 1, 2 * HD), F32),
            pltpu.SemaphoreType.DMA((beams,)),
        ],
    )(parents, start_dev, deep, shared)
    return attended, tail_out.reshape(tail_cache.shape)


def solution(mesh):
    placed = (
        P(None, None, "ctx"),
        P("ctx", "tp"),
        P("tp"),
        P("tp", "ctx"),
        P(None, "ctx", "tp"),
        P("ctx", None, None, "tp"),
        P(),
        P(),
    )
    return jax.shard_map(
        per_device,
        mesh=mesh,
        in_specs=placed,
        out_specs=(P(None, "tp", "ctx"), P("ctx", None, None, "tp")),
        check_vma=False,
    )
```

```python
import functools

import jax
import jax.numpy as jnp
import numpy as np
from jax import lax
from jax.experimental import pallas as pl
from jax.experimental.pallas import tpu as pltpu
from jax.sharding import PartitionSpec as P

HD = 128
BW = 8
GROUP = 8
STEPS = 2
ROWS = STEPS * BW
PAGE = 16
CTX = 64
POSITION = 17406
MIB = 1024 * 1024
F32, BF16 = jnp.float32, jnp.bfloat16

KEYS_AT, VALUES_AT, FRESH_AT, SENT = ROWS, ROWS + PAGE, ROWS + 2 * PAGE, ROWS + 2 * PAGE + BW
PACK = ROWS + 8
CARRY = ROWS + 2 * PAGE

VMEM = pl.BlockSpec(memory_space=pltpu.VMEM)
SMEM = pl.BlockSpec(memory_space=pltpu.SMEM)
HBM = pl.BlockSpec(memory_space=pltpu.HBM)


def rope_rows():
    half = HD // 2
    frequency = 1000000.0 ** (-(np.arange(half) * 2.0) / HD)
    table = np.zeros((8, HD), np.float32)
    for s in range(STEPS):
        angles = (POSITION + s) * frequency
        table[s] = np.concatenate([np.cos(angles), np.cos(angles)])
        table[STEPS + s] = np.concatenate([-np.sin(angles), np.sin(angles)])
    return table


def iota(shape, dim):
    return lax.broadcasted_iota(jnp.int32, shape, dim)


def project_kernel(
    parents_ref,
    start_ref,
    hidden_hbm,
    weight_hbm,
    bias_hbm,
    table_hbm,
    pages_hbm,
    out_ref,
    seen_ref,
    hidden_ref,
    weight_ref,
    bias_ref,
    table_ref,
    pages_ref,
    sems,
):
    me = lax.axis_index("ctx")
    pairs = (
        (hidden_hbm, hidden_ref),
        (weight_hbm, weight_ref),
        (bias_hbm, bias_ref),
        (table_hbm, table_ref),
        (pages_hbm, pages_ref),
    )
    copies = [pltpu.make_async_copy(a, b, sems.at[k]) for k, (a, b) in enumerate(pairs)]
    for copy in copies:
        copy.start()
    prompts = hidden_ref.shape[1] // BW
    beams = prompts * BW
    lane = iota((ROWS, HD), 1)
    row = iota((ROWS, HD), 0)

    for p in range(prompts):
        holder = jnp.zeros((ROWS, HD), jnp.int32)
        stale = lane < 0
        for b in range(BW):
            near = parents_ref[1, p * BW + b]
            holder = jnp.where(row == b, parents_ref[0, p * BW + b] - p * BW, holder)
            holder = jnp.where(row == BW + b, parents_ref[0, near] - p * BW, holder)
            last_page = ((me - start_ref[0, p * BW + b]) & (CTX - 1)) == CTX - 1
            cut = jnp.where(last_page, PAGE - STEPS, PAGE)
            stale = stale | ((lane // PAGE == b) & (lane % PAGE >= cut))
        old_seen = (lane // PAGE == holder) & jnp.logical_not(stale)
        seen_ref[p] = jnp.where(old_seen, 0.0, -jnp.inf)

    base = (me >> 3) * BW
    first_new = jnp.zeros((ROWS, HD), jnp.int32)
    for b in range(BW):
        first_new = jnp.where(row == b, b, first_new)
        first_new = jnp.where(row == BW + b, parents_ref[1, base + b] - base, first_new)
    second_new = jnp.where(row < BW, first_new, row)
    seen_ref[prompts] = jnp.where((lane == first_new) | (lane == second_new), 0.0, -jnp.inf)

    near = parents_ref[1, me]
    shift = (start_ref[2, me] - start_ref[0, parents_ref[0, near]]) & (CTX - 1)
    last = (start_ref[2, me] - 1) & (CTX - 1)
    facts = jnp.where(row == 0, shift, jnp.where(row == 1, last, near - base))
    seen_ref[prompts + 1] = facts.astype(F32)

    for copy in copies:
        copy.wait()
    for c in range(beams):
        far = parents_ref[0, parents_ref[1, c]]
        out_ref[c, KEYS_AT:VALUES_AT, :] = pages_ref[far, :, :HD]
        out_ref[c, VALUES_AT:FRESH_AT, :] = pages_ref[far, :, HD:]

    cosine = [jnp.broadcast_to(table_ref[s : s + 1], (BW, HD)) for s in range(STEPS)]
    sine = [jnp.broadcast_to(table_ref[STEPS + s : STEPS + s + 1], (BW, HD)) for s in range(STEPS)]
    cosine = jnp.concatenate(cosine * prompts, axis=0)
    sine = jnp.concatenate(sine * prompts, axis=0)
    steps = [hidden_ref[s].astype(F32) for s in range(STEPS)]
    rows = [steps[s][p * BW : (p + 1) * BW] for p in range(prompts) for s in range(STEPS)]
    hidden = jnp.concatenate(rows, axis=0).astype(BF16)
    bias = bias_ref[...].astype(F32) * (1.0 / CTX)
    for col in range(GROUP + 2):
        part = jnp.dot(
            hidden, weight_ref[:, col * HD : (col + 1) * HD], preferred_element_type=F32
        )
        part = part + bias[col : col + 1]
        if col <= GROUP:
            part = part * cosine + pltpu.roll(part, HD // 2, 1) * sine
        for p in range(prompts):
            tile = part[p * ROWS : (p + 1) * ROWS]
            if col < GROUP:
                out_ref[p * GROUP + col, :ROWS, :] = tile.astype(BF16)
            else:
                for h in range(GROUP):
                    if h % 2 == col - GROUP:
                        s = h // 2 % 2
                        out_ref[p * GROUP + h, FRESH_AT:, :] = tile[s * BW : (s + 1) * BW].astype(
                            BF16
                        )


def sum_kernel(parts_ref, out_ref, own_ref):
    query = jnp.sum(parts_ref[:, :ROWS, :].astype(F32), axis=0).astype(BF16)
    fresh = jnp.sum(parts_ref[:, FRESH_AT:, :].astype(F32), axis=0).astype(BF16)
    out_ref[...] = jnp.broadcast_to(query[None], out_ref.shape)
    own_ref[:ROWS, :] = query
    own_ref[ROWS:, :] = fresh


def attend_kernel(shared_ref, prefix_ref, pages_ref, seen_ref, own_ref, out_ref):
    h_me = lax.axis_index("ctx") & (GROUP - 1)
    prompts = prefix_ref.shape[0]
    scale = HD**-0.5
    contract = (((1,), (1,)), ((), ()))
    lane = iota((GROUP * ROWS, HD), 1)
    row = iota((GROUP * ROWS, HD), 0)
    slot = lane // ROWS
    diagonal = lane % ROWS == row % ROWS

    fresh = own_ref[ROWS:, :].astype(F32)
    fresh = jnp.where(h_me < GROUP // 2, pltpu.roll(fresh, 4, 0), fresh)
    line = iota((8, HD), 0)
    fresh = jnp.where(line >= 4, fresh, 0.0)

    def split(value):
        high = value.astype(BF16).astype(F32)
        rest = value - high
        mid = rest.astype(BF16).astype(F32)
        return high, mid, rest - mid

    for p in range(prompts):
        query = shared_ref[p * GROUP : (p + 1) * GROUP].reshape(GROUP * ROWS, HD)
        tail = pages_ref[p * BW : (p + 1) * BW].reshape(BW * PAGE, 2 * HD)
        s_pre = (
            lax.dot_general(query, prefix_ref[p, :, :HD], contract, preferred_element_type=F32)
            * scale
        )
        s_old = lax.dot_general(
            query, tail[:, :HD], contract, preferred_element_type=F32
        ) * scale + jnp.concatenate([seen_ref[p]] * GROUP, axis=0)
        peak = jnp.maximum(
            jnp.max(s_pre, axis=1, keepdims=True), jnp.max(s_old, axis=1, keepdims=True)
        )
        w_pre = jnp.exp(s_pre - peak)
        w_old = jnp.exp(s_old - peak)
        total = jnp.sum(w_pre, axis=1, keepdims=True) + jnp.sum(w_old, axis=1, keepdims=True)
        mixed = jnp.dot(
            w_pre.astype(BF16), prefix_ref[p, :, HD:], preferred_element_type=F32
        ) + jnp.dot(w_old.astype(BF16), tail[:, HD:], preferred_element_type=F32)
        out_ref[p * GROUP : (p + 1) * GROUP, :ROWS, :] = mixed.astype(BF16).reshape(
            GROUP, ROWS, HD
        )
        table = jnp.zeros((GROUP * ROWS, HD), F32)
        for k, term in enumerate(split(peak) + split(total)):
            table = jnp.where(slot == k, term, table)
        table = jnp.sum(jnp.where(diagonal, table, 0.0).reshape(GROUP, ROWS, HD), axis=1)
        for h in range(GROUP):
            out_ref[p * GROUP + h, ROWS:, :] = jnp.where(
                line == 0, table[h : h + 1], fresh
            ).astype(BF16)


def merge_kernel(parts_ref, own_ref, seen_ref, first_ref, out_ref):
    me = lax.axis_index("ctx")
    base = (me >> 3) * GROUP
    prompts = seen_ref.shape[0] - 2
    line = iota((8, HD), 0)

    def gather(kv):
        tiles = []
        for s in range(STEPS):
            low = parts_ref[base + 2 * s + kv, ROWS:, :].astype(F32)
            high = parts_ref[base + 2 * s + kv + GROUP // 2, ROWS:, :].astype(F32)
            tiles.append(jnp.where(line < 4, pltpu.roll(low, 4, 0), high))
        return tiles

    new_keys, new_values = gather(0), gather(1)
    blank = [jnp.zeros((HD - ROWS, HD), F32)]
    key = jnp.concatenate(new_keys + blank, axis=0).astype(BF16)
    value = jnp.concatenate(new_values + blank, axis=0).astype(BF16)
    s_new = (
        lax.dot_general(
            own_ref[:ROWS, :], key, (((1,), (1,)), ((), ())), preferred_element_type=F32
        )
        * HD**-0.5
        + seen_ref[prompts]
    )

    stats = parts_ref[:, ROWS:, :].astype(F32)
    stats = jnp.sum(jnp.where(iota(stats.shape, 1) == 0, stats, 0.0), axis=1)

    def term(k):
        return stats if k == 0 else pltpu.roll(stats, HD - k * ROWS, 1)

    def upright(table):
        return jnp.concatenate([table, jnp.zeros((HD - CTX, HD), F32)], axis=0).T[:ROWS]

    peak = upright(term(0) + term(1) + term(2))
    total = upright(term(3) + term(4) + term(5))
    peak = jnp.where(iota((ROWS, HD), 1) < CTX, peak, -jnp.inf)
    top = jnp.maximum(
        jnp.max(peak, axis=1, keepdims=True), jnp.max(s_new, axis=1, keepdims=True)
    )
    factor = jnp.exp(peak - top)
    w_new = jnp.exp(s_new - top)
    denominator = jnp.sum(total * factor + w_new, axis=1, keepdims=True)
    acc = jnp.dot(w_new.astype(BF16), value, preferred_element_type=F32)
    for k in range(CTX):
        acc = acc + factor[:, k : k + 1] * parts_ref[k, :ROWS, :].astype(F32)
    attention = (acc / denominator).astype(BF16)

    facts = seen_ref[prompts + 1]
    shift = jnp.max(facts[0:1]).astype(jnp.int32)
    last = jnp.max(facts[1:2]).astype(jnp.int32)
    for k in range(CTX):
        out_ref[k, :ROWS, :] = attention
        out_ref[k, ROWS:, :] = first_ref[(k - shift) & (CTX - 1), KEYS_AT:FRESH_AT, :]

    mine = (me & (BW - 1)).astype(F32)
    place = line.astype(F32)
    row = iota((PAGE, HD), 0)
    for at, tiles in ((ROWS, new_keys), (ROWS + PAGE, new_values)):
        earlier = jnp.sum(jnp.where(place == facts[2:3], tiles[0], 0.0), axis=0, keepdims=True)
        newest = jnp.sum(jnp.where(place == mine, tiles[1], 0.0), axis=0, keepdims=True)
        page = out_ref[last, at : at + PAGE, :].astype(F32)
        page = jnp.where(row == PAGE - 2, earlier, page)
        page = jnp.where(row == PAGE - 1, newest, page)
        out_ref[last, at : at + PAGE, :] = page.astype(BF16)


def output_kernel(heads_ref, weight_ref, out_ref):
    prompts = out_ref.shape[0]
    acc = jnp.zeros((prompts * ROWS, HD), F32)
    for h in range(GROUP):
        head = jnp.concatenate([heads_ref[p * GROUP + h, :ROWS, :] for p in range(prompts)], axis=0)
        acc = acc + jnp.dot(
            head, weight_ref[h * HD : (h + 1) * HD, :], preferred_element_type=F32
        )
    out_ref[...] = acc.astype(BF16).reshape(out_ref.shape)


def finish_kernel(share_ref, heads_hbm, out_ref, tail_hbm, sems):
    copies = [
        pltpu.make_async_copy(
            heads_hbm.at[:, pl.ds(ROWS + k * PAGE, PAGE), :],
            tail_hbm.at[:, :, pl.ds(k * HD, HD)],
            sems.at[k],
        )
        for k in range(2)
    ]
    for copy in copies:
        copy.start()
    total = jnp.sum(share_ref[...].astype(F32), axis=0)
    for s in range(STEPS):
        out_ref[s] = total[s * BW : (s + 1) * BW].astype(BF16)
    for copy in copies:
        copy.wait()


def call(kernel, shapes, in_specs, scratch=(), limit=32, out_specs=None):
    outs = [jax.ShapeDtypeStruct(shape, dtype) for shape, dtype in shapes]
    return pl.pallas_call(
        kernel,
        out_shape=outs,
        in_specs=in_specs,
        out_specs=out_specs or [VMEM] * len(outs),
        scratch_shapes=list(scratch),
        compiler_params=pltpu.CompilerParams(vmem_limit_bytes=limit * MIB),
    )


def per_device(
    hidden, qkv_weight, qkv_bias, out_weight, prefix_cache, tail_cache, parents, start_dev
):
    prompts = prefix_cache.shape[0]
    beams = prompts * BW
    pages = tail_cache.reshape(beams, PAGE, 2 * HD)
    bias = qkv_bias.reshape(GROUP + 2, HD)
    table = rope_rows()
    swap = functools.partial(lax.all_to_all, split_axis=0, concat_axis=0, tiled=True)

    parts, seen = call(
        project_kernel,
        [((CTX, SENT, HD), BF16), ((prompts + 2, ROWS, HD), F32)],
        [SMEM] * 2 + [HBM] * 5,
        [
            pltpu.VMEM(hidden.shape, BF16),
            pltpu.VMEM(qkv_weight.shape, BF16),
            pltpu.VMEM(bias.shape, BF16),
            pltpu.VMEM(table.shape, F32),
            pltpu.VMEM(pages.shape, BF16),
            pltpu.SemaphoreType.DMA((5,)),
        ],
        limit=60,
    )(parents, start_dev, hidden, qkv_weight, bias, table, pages)
    first = swap(parts, "ctx")
    mine, own = call(
        sum_kernel, [((CTX, ROWS, HD), BF16), ((ROWS + BW, HD), BF16)], [VMEM]
    )(first)
    shared = swap(mine, "ctx")
    (parts,) = call(attend_kernel, [((CTX, PACK, HD), BF16)], [VMEM] * 5)(
        shared, prefix_cache, pages, seen, own
    )
    parts = swap(parts, "ctx")
    (merged,) = call(merge_kernel, [((CTX, CARRY, HD), BF16)], [VMEM] * 4)(
        parts, own, seen, first
    )
    heads = swap(merged, "ctx")
    (share,) = call(output_kernel, [((prompts, ROWS, HD), BF16)], [VMEM] * 2)(heads, out_weight)
    share = swap(share, "tp")
    attended, tail_out = call(
        finish_kernel,
        [((STEPS, BW, HD), BF16), ((beams, PAGE, 2 * HD), BF16)],
        [VMEM, HBM],
        [pltpu.SemaphoreType.DMA((2,))],
        out_specs=[VMEM, HBM],
    )(share, heads)
    return attended, tail_out.reshape(tail_cache.shape)


def solution(mesh):
    placed = (
        P(None, None, "ctx"),
        P("ctx", "tp"),
        P("tp"),
        P("tp", "ctx"),
        P(None, "ctx", "tp"),
        P("ctx", None, None, "tp"),
        P(),
        P(),
    )
    return jax.shard_map(
        per_device,
        mesh=mesh,
        in_specs=placed,
        out_specs=(P(None, "tp", "ctx"), P("ctx", None, None, "tp")),
        check_vma=False,
    )
```

```python
import functools

import jax
import jax.numpy as jnp
import numpy as np
from jax import lax
from jax.experimental import pallas as pl
from jax.experimental.pallas import tpu as pltpu
from jax.sharding import PartitionSpec as P

HD = 128
BW = 8
GROUP = 8
STEPS = 2
ROWS = STEPS * BW
PAGE = 16
CTX = 64
POSITION = 17406
MIB = 1024 * 1024
F32, BF16 = jnp.float32, jnp.bfloat16

LX, LY, LC = 4, 8, 2
ALONG_XC = [[(x * LY + y) * LC + c for x in range(LX) for c in range(LC)] for y in range(LY)]
ALONG_Y = [[(x * LY + y) * LC + c for y in range(LY)] for x in range(LX) for c in range(LC)]

KEYS_AT, VALUES_AT, SHARE = GROUP * ROWS, (GROUP + 1) * ROWS, (GROUP + 2) * ROWS
STATS_AT, PACK = ROWS + 2 * PAGE, ROWS + 2 * PAGE + 8
CARRY = ROWS + 2 * PAGE

VMEM = pl.BlockSpec(memory_space=pltpu.VMEM)
SMEM = pl.BlockSpec(memory_space=pltpu.SMEM)
HBM = pl.BlockSpec(memory_space=pltpu.HBM)


def rope_rows():
    half = HD // 2
    frequency = 1000000.0 ** (-(np.arange(half) * 2.0) / HD)
    table = np.zeros((8, HD), np.float32)
    for s in range(STEPS):
        angles = (POSITION + s) * frequency
        table[s] = np.concatenate([np.cos(angles), np.cos(angles)])
        table[STEPS + s] = np.concatenate([-np.sin(angles), np.sin(angles)])
    return table


def iota(shape, dim):
    return lax.broadcasted_iota(jnp.int32, shape, dim)


def device_of(p, k):
    return (p // LC * LY + k) * LC + p % LC


def place():
    me = lax.axis_index("ctx")
    return me, (me >> 4) * LC + (me & 1), (me >> 1) & (LY - 1)


def project_kernel(
    parents_ref,
    start_ref,
    hidden_hbm,
    weight_hbm,
    bias_hbm,
    table_hbm,
    pages_hbm,
    out_ref,
    moved_ref,
    seen_ref,
    hidden_ref,
    weight_ref,
    bias_ref,
    table_ref,
    pages_ref,
    sems,
):
    me, prompt, beam = place()
    pairs = (
        (hidden_hbm, hidden_ref),
        (weight_hbm, weight_ref),
        (bias_hbm, bias_ref),
        (table_hbm, table_ref),
        (pages_hbm, pages_ref),
    )
    copies = [pltpu.make_async_copy(a, b, sems.at[k]) for k, (a, b) in enumerate(pairs)]
    for copy in copies:
        copy.start()
    prompts = hidden_ref.shape[1] // BW
    beams = prompts * BW
    lane = iota((ROWS, HD), 1)
    row = iota((ROWS, HD), 0)

    for p in range(prompts):
        holder = jnp.zeros((ROWS, HD), jnp.int32)
        stale = lane < 0
        for b in range(BW):
            near = parents_ref[1, p * BW + b]
            holder = jnp.where(row == b, parents_ref[0, p * BW + b] - p * BW, holder)
            holder = jnp.where(row == BW + b, parents_ref[0, near] - p * BW, holder)
            last_page = ((me - start_ref[0, p * BW + b]) & (CTX - 1)) == CTX - 1
            cut = jnp.where(last_page, PAGE - STEPS, PAGE)
            stale = stale | ((lane // PAGE == b) & (lane % PAGE >= cut))
        old_seen = (lane // PAGE == holder) & jnp.logical_not(stale)
        seen_ref[p] = jnp.where(old_seen, 0.0, -jnp.inf)

    base = prompt * BW
    first_new = jnp.zeros((ROWS, HD), jnp.int32)
    for b in range(BW):
        first_new = jnp.where(row == b, b, first_new)
        first_new = jnp.where(row == BW + b, parents_ref[1, base + b] - base, first_new)
    second_new = jnp.where(row < BW, first_new, row)
    seen_ref[prompts] = jnp.where((lane == first_new) | (lane == second_new), 0.0, -jnp.inf)

    near = parents_ref[1, base + beam]
    shift = (start_ref[2, base + beam] - start_ref[0, parents_ref[0, near]]) & (CTX - 1)
    last = (start_ref[2, base + beam] - 1) & (CTX - 1)
    facts = jnp.where(row == 0, shift, jnp.where(row == 1, last, near - base))
    seen_ref[prompts + 1] = facts.astype(F32)

    for copy in copies:
        copy.wait()
    for c in range(beams):
        far = parents_ref[0, parents_ref[1, c]]
        to = device_of(c // BW, c % BW)
        moved_ref[to, :PAGE, :] = pages_ref[far, :, :HD]
        moved_ref[to, PAGE:, :] = pages_ref[far, :, HD:]

    cosine = [jnp.broadcast_to(table_ref[s : s + 1], (BW, HD)) for s in range(STEPS)]
    sine = [jnp.broadcast_to(table_ref[STEPS + s : STEPS + s + 1], (BW, HD)) for s in range(STEPS)]
    cosine = jnp.concatenate(cosine * prompts, axis=0)
    sine = jnp.concatenate(sine * prompts, axis=0)
    steps = [hidden_ref[s].astype(F32) for s in range(STEPS)]
    rows = [steps[s][p * BW : (p + 1) * BW] for p in range(prompts) for s in range(STEPS)]
    hidden = jnp.concatenate(rows, axis=0).astype(BF16)
    bias = bias_ref[...].astype(F32) * (1.0 / CTX)
    for col in range(GROUP + 2):
        part = jnp.dot(
            hidden, weight_ref[:, col * HD : (col + 1) * HD], preferred_element_type=F32
        )
        part = part + bias[col : col + 1]
        if col <= GROUP:
            part = part * cosine + pltpu.roll(part, HD // 2, 1) * sine
        part = part.astype(BF16)
        for p in range(prompts):
            out_ref[p, col * ROWS : (col + 1) * ROWS, :] = part[p * ROWS : (p + 1) * ROWS]


def row_sum_kernel(parts_ref, out_ref):
    total = jnp.sum(parts_ref[...].astype(F32), axis=0).astype(BF16)
    out_ref[...] = jnp.broadcast_to(total[None], out_ref.shape)


def sum_kernel(parts_ref, out_ref, own_ref):
    total = jnp.sum(parts_ref[...].astype(F32), axis=0).astype(BF16)
    out_ref[...] = jnp.broadcast_to(total[None, :KEYS_AT], out_ref.shape)
    own_ref[...] = total


def attend_kernel(shared_ref, prefix_ref, pages_ref, seen_ref, moved_ref, out_ref):
    prompts = prefix_ref.shape[0]
    scale = HD**-0.5
    contract = (((1,), (1,)), ((), ()))
    lane = iota((GROUP * ROWS, HD), 1)
    row = iota((GROUP * ROWS, HD), 0)
    slot = lane // ROWS
    diagonal = lane % ROWS == row % ROWS
    line = iota((8, HD), 0)

    def split(value):
        high = value.astype(BF16).astype(F32)
        rest = value - high
        mid = rest.astype(BF16).astype(F32)
        return high, mid, rest - mid

    for p in range(prompts):
        query = shared_ref[p]
        tail = pages_ref[p * BW : (p + 1) * BW].reshape(BW * PAGE, 2 * HD)
        s_pre = (
            lax.dot_general(query, prefix_ref[p, :, :HD], contract, preferred_element_type=F32)
            * scale
        )
        s_old = lax.dot_general(
            query, tail[:, :HD], contract, preferred_element_type=F32
        ) * scale + jnp.concatenate([seen_ref[p]] * GROUP, axis=0)
        peak = jnp.maximum(
            jnp.max(s_pre, axis=1, keepdims=True), jnp.max(s_old, axis=1, keepdims=True)
        )
        w_pre = jnp.exp(s_pre - peak)
        w_old = jnp.exp(s_old - peak)
        total = jnp.sum(w_pre, axis=1, keepdims=True) + jnp.sum(w_old, axis=1, keepdims=True)
        mixed = jnp.dot(
            w_pre.astype(BF16), prefix_ref[p, :, HD:], preferred_element_type=F32
        ) + jnp.dot(w_old.astype(BF16), tail[:, HD:], preferred_element_type=F32)
        mixed = mixed.astype(BF16)
        table = jnp.zeros((GROUP * ROWS, HD), F32)
        for k, term in enumerate(split(peak) + split(total)):
            table = jnp.where(slot == k, term, table)
        table = jnp.sum(jnp.where(diagonal, table, 0.0).reshape(GROUP, ROWS, HD), axis=1)
        for h in range(GROUP):
            to = device_of(p, h)
            out_ref[to, :ROWS, :] = mixed[h * ROWS : (h + 1) * ROWS]
            out_ref[to, ROWS:STATS_AT, :] = moved_ref[to]
            out_ref[to, STATS_AT:, :] = jnp.where(line == 0, table[h : h + 1], 0.0).astype(BF16)


def merge_kernel(parts_ref, own_ref, seen_ref, out_ref):
    _, _, beam = place()
    prompts = seen_ref.shape[0] - 2

    blank = jnp.zeros((HD - ROWS, HD), BF16)
    key = jnp.concatenate([own_ref[KEYS_AT:VALUES_AT, :], blank], axis=0)
    value = jnp.concatenate([own_ref[VALUES_AT:, :], blank], axis=0)
    query = own_ref[pl.ds(pl.multiple_of(beam * ROWS, ROWS), ROWS), :]
    s_new = (
        lax.dot_general(query, key, (((1,), (1,)), ((), ())), preferred_element_type=F32)
        * HD**-0.5
        + seen_ref[prompts]
    )

    stats = parts_ref[:, STATS_AT:, :].astype(F32)
    stats = jnp.sum(jnp.where(iota(stats.shape, 1) == 0, stats, 0.0), axis=1)

    def term(k):
        return stats if k == 0 else pltpu.roll(stats, HD - k * ROWS, 1)

    def upright(table):
        return jnp.concatenate([table, jnp.zeros((HD - CTX, HD), F32)], axis=0).T[:ROWS]

    peak = upright(term(0) + term(1) + term(2))
    total = upright(term(3) + term(4) + term(5))
    peak = jnp.where(iota((ROWS, HD), 1) < CTX, peak, -jnp.inf)
    top = jnp.maximum(
        jnp.max(peak, axis=1, keepdims=True), jnp.max(s_new, axis=1, keepdims=True)
    )
    factor = jnp.exp(peak - top)
    w_new = jnp.exp(s_new - top)
    denominator = jnp.sum(total * factor + w_new, axis=1, keepdims=True)
    acc = jnp.dot(w_new.astype(BF16), value, preferred_element_type=F32)
    for k in range(CTX):
        acc = acc + factor[:, k : k + 1] * parts_ref[k, :ROWS, :].astype(F32)
    attention = (acc / denominator).astype(BF16)

    facts = seen_ref[prompts + 1]
    shift = jnp.max(facts[0:1]).astype(jnp.int32)
    last = jnp.max(facts[1:2]).astype(jnp.int32)
    for k in range(CTX):
        out_ref[k, :ROWS, :] = attention
        out_ref[k, ROWS:, :] = parts_ref[(k - shift) & (CTX - 1), ROWS:STATS_AT, :]

    row = iota((PAGE, HD), 0)
    line = row.astype(F32)
    mine = (BW + beam).astype(F32)
    for at, rows in ((ROWS, key), (ROWS + PAGE, value)):
        rows = rows[:ROWS].astype(F32)
        earlier = jnp.sum(jnp.where(line == facts[2:3], rows, 0.0), axis=0, keepdims=True)
        newest = jnp.sum(jnp.where(line == mine, rows, 0.0), axis=0, keepdims=True)
        page = out_ref[last, at : at + PAGE, :].astype(F32)
        page = jnp.where(row == PAGE - 2, earlier, page)
        page = jnp.where(row == PAGE - 1, newest, page)
        out_ref[last, at : at + PAGE, :] = page.astype(BF16)


def output_kernel(heads_ref, weight_ref, out_ref):
    prompts = out_ref.shape[0]
    acc = jnp.zeros((prompts * ROWS, HD), F32)
    for h in range(GROUP):
        head = [heads_ref[device_of(p, h), :ROWS, :] for p in range(prompts)]
        head = jnp.concatenate(head, axis=0)
        acc = acc + jnp.dot(
            head, weight_ref[h * HD : (h + 1) * HD, :], preferred_element_type=F32
        )
    out_ref[...] = acc.astype(BF16).reshape(out_ref.shape)


def finish_kernel(share_ref, heads_hbm, out_ref, tail_hbm, sems):
    copies = []
    for core in range(LC):
        for k in range(2):
            copies.append(
                pltpu.make_async_copy(
                    heads_hbm.at[:, :, core, pl.ds(ROWS + k * PAGE, PAGE), :],
                    tail_hbm.at[:, core, :, :, pl.ds(k * HD, HD)],
                    sems.at[2 * core + k],
                )
            )
    for copy in copies:
        copy.start()
    total = jnp.sum(share_ref[...].astype(F32), axis=0)
    for s in range(STEPS):
        out_ref[s] = total[s * BW : (s + 1) * BW].astype(BF16)
    for copy in copies:
        copy.wait()


def call(kernel, shapes, in_specs, scratch=(), limit=32, out_specs=None):
    outs = [jax.ShapeDtypeStruct(shape, dtype) for shape, dtype in shapes]
    return pl.pallas_call(
        kernel,
        out_shape=outs,
        in_specs=in_specs,
        out_specs=out_specs or [VMEM] * len(outs),
        scratch_shapes=list(scratch),
        compiler_params=pltpu.CompilerParams(vmem_limit_bytes=limit * MIB),
    )


def per_device(
    hidden, qkv_weight, qkv_bias, out_weight, prefix_cache, tail_cache, parents, start_dev
):
    prompts = prefix_cache.shape[0]
    beams = prompts * BW
    pages = tail_cache.reshape(beams, PAGE, 2 * HD)
    bias = qkv_bias.reshape(GROUP + 2, HD)
    table = rope_rows()
    swap = functools.partial(
        lax.all_to_all, axis_name="ctx", split_axis=0, concat_axis=0, tiled=True
    )

    parts, moved, seen = call(
        project_kernel,
        [
            ((prompts, SHARE, HD), BF16),
            ((CTX, 2 * PAGE, HD), BF16),
            ((prompts + 2, ROWS, HD), F32),
        ],
        [SMEM] * 2 + [HBM] * 5,
        [
            pltpu.VMEM(hidden.shape, BF16),
            pltpu.VMEM(qkv_weight.shape, BF16),
            pltpu.VMEM(bias.shape, BF16),
            pltpu.VMEM(table.shape, F32),
            pltpu.VMEM(pages.shape, BF16),
            pltpu.SemaphoreType.DMA((5,)),
        ],
        limit=60,
    )(parents, start_dev, hidden, qkv_weight, bias, table, pages)
    parts = swap(parts, axis_index_groups=ALONG_XC)
    (parts,) = call(row_sum_kernel, [((LY, SHARE, HD), BF16)], [VMEM])(parts)
    parts = swap(parts, axis_index_groups=ALONG_Y)
    mine, own = call(
        sum_kernel, [((prompts, KEYS_AT, HD), BF16), ((SHARE, HD), BF16)], [VMEM]
    )(parts)
    shared = swap(mine, axis_index_groups=ALONG_XC)
    (parts,) = call(attend_kernel, [((CTX, PACK, HD), BF16)], [VMEM] * 5)(
        shared, prefix_cache, pages, seen, moved
    )
    parts = swap(parts)
    (merged,) = call(merge_kernel, [((CTX, CARRY, HD), BF16)], [VMEM] * 3)(parts, own, seen)
    heads = swap(merged)
    (share,) = call(output_kernel, [((prompts, ROWS, HD), BF16)], [VMEM] * 2)(heads, out_weight)
    share = swap(share, axis_name="tp")
    attended, tail_out = call(
        finish_kernel,
        [((STEPS, BW, HD), BF16), ((LX, LC, LY, PAGE, 2 * HD), BF16)],
        [VMEM, HBM],
        [pltpu.SemaphoreType.DMA((4,))],
        out_specs=[VMEM, HBM],
    )(share, heads.reshape(LX, LY, LC, CARRY, HD))
    return attended, tail_out.reshape(tail_cache.shape)


def solution(mesh):
    placed = (
        P(None, None, "ctx"),
        P("ctx", "tp"),
        P("tp"),
        P("tp", "ctx"),
        P(None, "ctx", "tp"),
        P("ctx", None, None, "tp"),
        P(),
        P(),
    )
    return jax.shard_map(
        per_device,
        mesh=mesh,
        in_specs=placed,
        out_specs=(P(None, "tp", "ctx"), P("ctx", None, None, "tp")),
        check_vma=False,
    )
```

```python
import functools

import jax
import jax.numpy as jnp
import numpy as np
from jax import lax
from jax.experimental import pallas as pl
from jax.experimental.pallas import tpu as pltpu
from jax.sharding import PartitionSpec as P

HD = 128
BW = 8
GROUP = 8
STEPS = 2
ROWS = STEPS * BW
PAGE = 16
CTX = 64
POSITION = 17406
MIB = 1024 * 1024
F32, BF16 = jnp.float32, jnp.bfloat16

LX, LY, LC = 4, 8, 2
ALONG_XC = [[(x * LY + y) * LC + c for x in range(LX) for c in range(LC)] for y in range(LY)]
ALONG_Y = [[(x * LY + y) * LC + c for y in range(LY)] for x in range(LX) for c in range(LC)]

KEYS_AT, VALUES_AT, SHARE = GROUP * ROWS, (GROUP + 1) * ROWS, (GROUP + 2) * ROWS
STATS_AT, PACK = ROWS + LX * LC * 2 * PAGE, ROWS + LX * LC * 2 * PAGE + 8
CARRY = ROWS + 2 * PAGE

VMEM = pl.BlockSpec(memory_space=pltpu.VMEM)
SMEM = pl.BlockSpec(memory_space=pltpu.SMEM)
HBM = pl.BlockSpec(memory_space=pltpu.HBM)


def rope_rows():
    half = HD // 2
    frequency = 1000000.0 ** (-(np.arange(half) * 2.0) / HD)
    table = np.zeros((8, HD), np.float32)
    for s in range(STEPS):
        angles = (POSITION + s) * frequency
        table[s] = np.concatenate([np.cos(angles), np.cos(angles)])
        table[STEPS + s] = np.concatenate([-np.sin(angles), np.sin(angles)])
    return table


def iota(shape, dim):
    return lax.broadcasted_iota(jnp.int32, shape, dim)


def device_of(p, k):
    return (p // LC * LY + k) * LC + p % LC


def place():
    me = lax.axis_index("ctx")
    return me, (me >> 4) * LC + (me & 1), (me >> 1) & (LY - 1)


def project_kernel(
    parents_ref,
    start_ref,
    hidden_hbm,
    weight_hbm,
    bias_hbm,
    table_hbm,
    prefix_hbm,
    pages_hbm,
    out_ref,
    seen_ref,
    pick_ref,
    hidden_ref,
    weight_ref,
    bias_ref,
    table_ref,
    sems,
):
    pairs = [
        (hidden_hbm, hidden_ref),
        (weight_hbm, weight_ref),
        (bias_hbm, bias_ref),
        (table_hbm, table_ref),
    ]
    needed = len(pairs)
    prompts, tokens = prefix_hbm.shape[:2]
    tail = BW * PAGE
    for p in range(prompts):
        at = SHARE
        for source, count in (
            (prefix_hbm.at[p], tokens),
            (pages_hbm.at[pl.ds(p * tail, tail)], tail),
        ):
            for k in range(2):
                lanes = source.at[:, pl.ds(k * HD, HD)]
                pairs.append((lanes, out_ref.at[p, pl.ds(at, count), :]))
                at += count
    copies = [pltpu.make_async_copy(a, b, sems.at[k]) for k, (a, b) in enumerate(pairs)]
    for copy in copies:
        copy.start()

    _, prompt, beam = place()
    base = prompt * BW
    lane = iota((ROWS, HD), 1)
    row = iota((ROWS, HD), 0)
    holder = jnp.zeros((ROWS, HD), jnp.int32)
    first = jnp.zeros((ROWS, HD), jnp.int32)
    for b in range(BW):
        near = parents_ref[1, base + b]
        holder = jnp.where(row == b, parents_ref[0, base + b] - base, holder)
        holder = jnp.where(row == BW + b, parents_ref[0, near] - base, holder)
        first = jnp.where(lane // PAGE == b, start_ref[0, base + b], first)
    for u in range(LX * LC):
        device = (u // LC * LY + beam) * LC + u % LC
        last_page = ((device - first) & (CTX - 1)) == CTX - 1
        stale = last_page & (lane % PAGE >= PAGE - STEPS)
        old_seen = (lane // PAGE == holder) & jnp.logical_not(stale)
        seen_ref[u] = jnp.where(old_seen, 0.0, -jnp.inf)

    first_new = jnp.zeros((ROWS, HD), jnp.int32)
    for b in range(BW):
        first_new = jnp.where(row == b, b, first_new)
        first_new = jnp.where(row == BW + b, parents_ref[1, base + b] - base, first_new)
    second_new = jnp.where(row < BW, first_new, row)
    seen_ref[LX * LC] = jnp.where((lane == first_new) | (lane == second_new), 0.0, -jnp.inf)

    near = parents_ref[1, base + beam]
    shift = (start_ref[2, base + beam] - start_ref[0, parents_ref[0, near]]) & (CTX - 1)
    last = (start_ref[2, base + beam] - 1) & (CTX - 1)
    facts = jnp.where(row == 0, shift, jnp.where(row == 1, last, near - base))
    seen_ref[LX * LC + 1] = facts.astype(F32)

    lane = iota((tail, HD), 1)
    row = iota((tail, HD), 0)
    wanted = jnp.zeros((tail, HD), jnp.int32)
    for b in range(BW):
        far = parents_ref[0, parents_ref[1, base + b]] - base
        wanted = jnp.where(row // PAGE == b, far * PAGE + row % PAGE, wanted)
    pick_ref[...] = jnp.where(lane == wanted, 1.0, 0.0).astype(BF16)

    for copy in copies[:needed]:
        copy.wait()
    cosine = [jnp.broadcast_to(table_ref[s : s + 1], (BW, HD)) for s in range(STEPS)]
    sine = [jnp.broadcast_to(table_ref[STEPS + s : STEPS + s + 1], (BW, HD)) for s in range(STEPS)]
    cosine = jnp.concatenate(cosine * prompts, axis=0)
    sine = jnp.concatenate(sine * prompts, axis=0)
    steps = [hidden_ref[s].astype(F32) for s in range(STEPS)]
    rows = [steps[s][p * BW : (p + 1) * BW] for p in range(prompts) for s in range(STEPS)]
    hidden = jnp.concatenate(rows, axis=0).astype(BF16)
    bias = bias_ref[...].astype(F32) * (1.0 / CTX)
    for col in range(GROUP + 2):
        part = jnp.dot(
            hidden, weight_ref[:, col * HD : (col + 1) * HD], preferred_element_type=F32
        )
        part = part + bias[col : col + 1]
        if col <= GROUP:
            part = part * cosine + pltpu.roll(part, HD // 2, 1) * sine
        part = part.astype(BF16)
        for p in range(prompts):
            out_ref[p, col * ROWS : (col + 1) * ROWS, :] = part[p * ROWS : (p + 1) * ROWS]
    for copy in copies[needed:]:
        copy.wait()


def row_sum_kernel(parts_ref, out_ref):
    total = jnp.sum(parts_ref[:, :SHARE, :].astype(F32), axis=0).astype(BF16)
    out_ref[...] = jnp.broadcast_to(total[None], out_ref.shape)


def attend_kernel(sums_ref, cache_ref, seen_ref, pick_ref, out_ref, own_ref, score_ref):
    chunks = cache_ref.shape[0]
    tail = BW * PAGE
    tokens = (cache_ref.shape[1] - SHARE) // 2 - tail
    v_at, tk_at = SHARE + tokens, SHARE + 2 * tokens
    tv_at = tk_at + tail
    scale = HD**-0.5
    contract = (((1,), (1,)), ((), ()))
    lane = iota((GROUP * ROWS, HD), 1)
    row = iota((GROUP * ROWS, HD), 0)
    slot = lane // ROWS
    diagonal = lane % ROWS == row % ROWS
    line = iota((8, HD), 0)

    def split(value):
        high = value.astype(BF16).astype(F32)
        rest = value - high
        mid = rest.astype(BF16).astype(F32)
        return high, mid, rest - mid

    total = jnp.sum(sums_ref[...].astype(F32), axis=0).astype(BF16)
    own_ref[...] = total
    query = total[:KEYS_AT]
    peak = jnp.full((GROUP * ROWS, HD), -jnp.inf, F32)
    for u in range(chunks):
        keys = cache_ref[u, SHARE:v_at, :]
        score = lax.dot_general(query, keys, contract, preferred_element_type=F32) * scale
        score_ref[u, :, :tokens] = score
        for k in range(0, tokens, HD):
            peak = jnp.maximum(peak, score[:, k : k + HD])
        keys = cache_ref[u, tk_at:tv_at, :]
        score = lax.dot_general(query, keys, contract, preferred_element_type=F32) * scale
        score = score + jnp.concatenate([seen_ref[u]] * GROUP, axis=0)
        score_ref[u, :, tokens:] = score
        peak = jnp.maximum(peak, score)
    peak = jnp.max(peak, axis=1, keepdims=True)
    total = jnp.zeros((GROUP * ROWS, HD), F32)
    mixed = jnp.zeros((GROUP * ROWS, HD), F32)
    for u in range(chunks):
        weight = jnp.exp(score_ref[u] - peak)
        for k in range(0, tokens + tail, HD):
            total = total + weight[:, k : k + HD]
        weight = weight.astype(BF16)
        mixed = mixed + jnp.dot(
            weight[:, :tokens], cache_ref[u, v_at:tk_at, :], preferred_element_type=F32
        )
        mixed = mixed + jnp.dot(
            weight[:, tokens:], cache_ref[u, tv_at:, :], preferred_element_type=F32
        )
    total = jnp.sum(total, axis=1, keepdims=True)
    mixed = mixed.astype(BF16)

    table = jnp.zeros((GROUP * ROWS, HD), F32)
    for k, term in enumerate(split(peak) + split(total)):
        table = jnp.where(slot == k, term, table)
    table = jnp.sum(jnp.where(diagonal, table, 0.0).reshape(GROUP, ROWS, HD), axis=1)
    for h in range(GROUP):
        out_ref[h, :ROWS, :] = mixed[h * ROWS : (h + 1) * ROWS]
        out_ref[h, STATS_AT:, :] = jnp.where(line == 0, table[h : h + 1], 0.0).astype(BF16)

    for u in range(chunks):
        for k, at in enumerate((tk_at, tv_at)):
            moved = jnp.dot(pick_ref[...], cache_ref[u, at : at + tail, :], preferred_element_type=F32)
            moved = moved.astype(BF16)
            for b in range(BW):
                to = ROWS + (2 * u + k) * PAGE
                out_ref[b, to : to + PAGE, :] = moved[b * PAGE : (b + 1) * PAGE]


def merge_kernel(parts_ref, own_ref, seen_ref, out_ref):
    _, _, beam = place()
    masks = seen_ref.shape[0] - 2

    blank = jnp.zeros((HD - ROWS, HD), BF16)
    key = jnp.concatenate([own_ref[KEYS_AT:VALUES_AT, :], blank], axis=0)
    value = jnp.concatenate([own_ref[VALUES_AT:, :], blank], axis=0)
    query = own_ref[pl.ds(pl.multiple_of(beam * ROWS, ROWS), ROWS), :]
    s_new = (
        lax.dot_general(query, key, (((1,), (1,)), ((), ())), preferred_element_type=F32)
        * HD**-0.5
        + seen_ref[masks]
    )

    stats = parts_ref[:, STATS_AT:, :].astype(F32)
    stats = jnp.sum(jnp.where(iota(stats.shape, 1) == 0, stats, 0.0), axis=1)

    def term(k):
        return stats if k == 0 else pltpu.roll(stats, HD - k * ROWS, 1)

    def upright(table):
        return jnp.concatenate([table, jnp.zeros((HD - LY, HD), F32)], axis=0).T[:ROWS]

    peak = upright(term(0) + term(1) + term(2))
    total = upright(term(3) + term(4) + term(5))
    peak = jnp.where(iota((ROWS, HD), 1) < LY, peak, -jnp.inf)
    top = jnp.maximum(
        jnp.max(peak, axis=1, keepdims=True), jnp.max(s_new, axis=1, keepdims=True)
    )
    factor = jnp.exp(peak - top)
    w_new = jnp.exp(s_new - top)
    denominator = jnp.sum(total * factor + w_new, axis=1, keepdims=True)
    acc = jnp.dot(w_new.astype(BF16), value, preferred_element_type=F32)
    for k in range(LY):
        acc = acc + factor[:, k : k + 1] * parts_ref[k, :ROWS, :].astype(F32)
    attention = (acc / denominator).astype(BF16)

    facts = seen_ref[masks + 1]
    shift = jnp.max(facts[0:1]).astype(jnp.int32)
    last = jnp.max(facts[1:2]).astype(jnp.int32)
    for k in range(CTX):
        out_ref[k, :ROWS, :] = attention
        held = (k - shift) & (CTX - 1)
        column = (held >> 4) * LC + (held & 1)
        at = pl.multiple_of(ROWS + column * 2 * PAGE, PAGE)
        out_ref[k, ROWS:, :] = parts_ref[(held >> 1) & (LY - 1), pl.ds(at, 2 * PAGE), :]

    row = iota((PAGE, HD), 0)
    line = row.astype(F32)
    mine = (BW + beam).astype(F32)
    for at, rows in ((ROWS, key), (ROWS + PAGE, value)):
        rows = rows[:ROWS].astype(F32)
        earlier = jnp.sum(jnp.where(line == facts[2:3], rows, 0.0), axis=0, keepdims=True)
        newest = jnp.sum(jnp.where(line == mine, rows, 0.0), axis=0, keepdims=True)
        page = out_ref[last, at : at + PAGE, :].astype(F32)
        page = jnp.where(row == PAGE - 2, earlier, page)
        page = jnp.where(row == PAGE - 1, newest, page)
        out_ref[last, at : at + PAGE, :] = page.astype(BF16)


def output_kernel(heads_ref, weight_ref, out_ref):
    prompts = out_ref.shape[0]
    acc = jnp.zeros((prompts * ROWS, HD), F32)
    for h in range(GROUP):
        head = [heads_ref[device_of(p, h), :ROWS, :] for p in range(prompts)]
        head = jnp.concatenate(head, axis=0)
        acc = acc + jnp.dot(
            head, weight_ref[h * HD : (h + 1) * HD, :], preferred_element_type=F32
        )
    out_ref[...] = acc.astype(BF16).reshape(out_ref.shape)


def finish_kernel(share_ref, heads_hbm, out_ref, tail_hbm, sems):
    copies = []
    for core in range(LC):
        for k in range(2):
            copies.append(
                pltpu.make_async_copy(
                    heads_hbm.at[:, :, core, pl.ds(ROWS + k * PAGE, PAGE), :],
                    tail_hbm.at[:, core, :, :, pl.ds(k * HD, HD)],
                    sems.at[2 * core + k],
                )
            )
    for copy in copies:
        copy.start()
    total = jnp.sum(share_ref[...].astype(F32), axis=0)
    for s in range(STEPS):
        out_ref[s] = total[s * BW : (s + 1) * BW].astype(BF16)
    for copy in copies:
        copy.wait()


def call(kernel, shapes, in_specs, scratch=(), limit=32, out_specs=None):
    outs = [jax.ShapeDtypeStruct(shape, dtype) for shape, dtype in shapes]
    return pl.pallas_call(
        kernel,
        out_shape=outs,
        in_specs=in_specs,
        out_specs=out_specs or [VMEM] * len(outs),
        scratch_shapes=list(scratch),
        compiler_params=pltpu.CompilerParams(vmem_limit_bytes=limit * MIB),
    )


def per_device(
    hidden, qkv_weight, qkv_bias, out_weight, prefix_cache, tail_cache, parents, start_dev
):
    prompts = prefix_cache.shape[0]
    beams = prompts * BW
    bias = qkv_bias.reshape(GROUP + 2, HD)
    table = rope_rows()
    swap = functools.partial(
        lax.all_to_all, axis_name="ctx", split_axis=0, concat_axis=0, tiled=True
    )

    tail = BW * PAGE
    load = SHARE + 2 * prefix_cache.shape[1] + 2 * tail
    parts, seen, pick = call(
        project_kernel,
        [
            ((prompts, load, HD), BF16),
            ((LX * LC + 2, ROWS, HD), F32),
            ((tail, HD), BF16),
        ],
        [SMEM] * 2 + [HBM] * 6,
        [
            pltpu.VMEM(hidden.shape, BF16),
            pltpu.VMEM(qkv_weight.shape, BF16),
            pltpu.VMEM(bias.shape, BF16),
            pltpu.VMEM(table.shape, F32),
            pltpu.SemaphoreType.DMA((4 + 4 * prompts,)),
        ],
        limit=60,
    )(
        parents,
        start_dev,
        hidden,
        qkv_weight,
        bias,
        table,
        prefix_cache,
        tail_cache.reshape(beams * PAGE, 2 * HD),
    )
    cache = swap(parts, axis_index_groups=ALONG_XC)
    (parts,) = call(row_sum_kernel, [((LY, SHARE, HD), BF16)], [VMEM])(cache)
    sums = swap(parts, axis_index_groups=ALONG_Y)
    parts, own = call(
        attend_kernel,
        [((LY, PACK, HD), BF16), ((SHARE, HD), BF16)],
        [VMEM] * 4,
        [pltpu.VMEM((prompts, KEYS_AT, prefix_cache.shape[1] + tail), F32)],
    )(sums, cache, seen, pick)
    parts = swap(parts, axis_index_groups=ALONG_Y)
    (merged,) = call(merge_kernel, [((CTX, CARRY, HD), BF16)], [VMEM] * 3)(parts, own, seen)
    heads = swap(merged)
    (share,) = call(output_kernel, [((prompts, ROWS, HD), BF16)], [VMEM] * 2)(heads, out_weight)
    share = swap(share, axis_name="tp")
    attended, tail_out = call(
        finish_kernel,
        [((STEPS, BW, HD), BF16), ((LX, LC, LY, PAGE, 2 * HD), BF16)],
        [VMEM, HBM],
        [pltpu.SemaphoreType.DMA((4,))],
        out_specs=[VMEM, HBM],
    )(share, heads.reshape(LX, LY, LC, CARRY, HD))
    return attended, tail_out.reshape(tail_cache.shape)


def solution(mesh):
    placed = (
        P(None, None, "ctx"),
        P("ctx", "tp"),
        P("tp"),
        P("tp", "ctx"),
        P(None, "ctx", "tp"),
        P("ctx", None, None, "tp"),
        P(),
        P(),
    )
    return jax.shard_map(
        per_device,
        mesh=mesh,
        in_specs=placed,
        out_specs=(P(None, "tp", "ctx"), P("ctx", None, None, "tp")),
        check_vma=False,
    )
```
